32 devices in a mesh: fsdp: 16 (over z, y, x), dp: 2 (over core).
Axes of the slice: x: 2, y: 2, z: 4, core: 2. Of those that a mesh axis runs over, the one named last changes fastest.
Arguments:
- tokens: bfloat16 [4096, 8192], P(('fsdp', 'dp')), may hold values from -6 to 6
- token_adapter_index: int32 [4096, 1], P(('fsdp', 'dp')), may hold values from 0 to 15; in each aligned block of 128 rows (0 to 127, 128 to 255, ...) at most 12 rows name the same one
- adapter_storage_index: int32 [16], replicated, may hold values from 0 to 15, each once
- frozen_value_weight: bfloat16 [8192, 512], P(('fsdp', 'dp')), may hold values from -0.0625 to 0.0625
- frozen_value_bias: bfloat16 [512], replicated, may hold values from -3 to 3
- adapter_down_weight: bfloat16 [16, 8192, 64], P('fsdp'), may hold values from -0.0625 to 0.0625
- adapter_up_weight: bfloat16 [16, 64, 512], P('fsdp'), may hold values from -0.75 to 0.75
- cotangent: bfloat16 [4096, 512], P(('fsdp', 'dp')), may hold values from -0.1875 to 0.1875
Outputs:
- values: bfloat16 [4096, 512], P(('fsdp', 'dp'))
- grad_down: float32 [16, 8192, 64], P('fsdp', 'dp')
- grad_up: float32 [16, 64, 512], P('fsdp', None, 'dp')
The draws below stay inside these ranges and needn't reach their ends.
Inputs may be any that keep to these rules, and one draw needn't show every extreme that they name: `token_adapter_index`: within the 128 rows of one device no adapter is named by more than 12 rows. `adapter_storage_index`: each storage index appears once.
All inputs are finite; a program needn't handle non-finite values.
Results may differ from the reference program's by a relative error of at most 0.0048.
Values may be sent and summed in bfloat16 or wider, within the bound.
A program may use at most 64 MiB of HBM per device.

```python
import math
import jax
import jax.numpy as jnp
import numpy as np
from jax import lax

MODEL_DIM = 8192
VALUE_OUT_WIDTH = 512
ADAPTER_RANK = 64
TOK_DEV = 128
TOKENS = 4096
ADAPTER_COUNT = 16
CAP = 12
N_FSDP = 16
N_DP = 2


def levels(own_key, shape, shards, smallest, high):
    gain = 1.0
    for position, parts in shards:
        steps = jax.random.uniform(jax.random.fold_in(jax.random.fold_in(own_key, 6), position), (parts,), jnp.float32, smallest / len(shards), high / len(shards))
        gain = gain * jnp.repeat(jnp.exp(steps), shape[position] // parts).reshape((-1,) + (1,) * (len(shape) - 1 - position))
    return gain


def deal_out(own_key, own, number, rows, number_of, top, limit, skew):
    ranking = jax.random.permutation(own_key, number_of)
    crowded, common = shares(number_of, rows * top, limit, skew, True), shares(number_of, rows * top, limit, skew, False)
    places = jnp.arange(number_of)

    def named(lengths, rotation):
        used = int((lengths > 0).sum())
        fixed = max(1, used // 4)
        moved = fixed + (places - fixed + rotation * (used - fixed)) % max(1, number_of - fixed)
        return jnp.zeros((number_of,), jnp.int32).at[ranking[jnp.where(places < fixed, places, moved)]].set(jnp.asarray(lengths, jnp.int32))

    lengths = jnp.where(number % 4 == 0, named(crowded, number // 4), named(common, number - number // 4 - 1))
    mixed = jax.random.permutation(jax.random.fold_in(own, 3), number_of)
    source_of, sink = mixed[0:number_of // 2 * 2:2], mixed[1:number_of // 2 * 2:2]
    margin = jnp.minimum(lengths[source_of] - 1, limit - lengths[sink]) // 2
    margin = jnp.where((source_of == ranking[0]) | (sink == ranking[0]) | (lengths[sink] == 0), 0, jnp.maximum(margin, 0))
    moved = jax.random.randint(jax.random.fold_in(own, 4), (number_of // 2,), 0, 1 << 20) % (margin + 1)
    lengths = lengths.at[source_of].add(-moved).at[sink].add(moved)
    labels = jnp.searchsorted(jnp.cumsum(lengths), jnp.arange(rows * top), side="right").astype(jnp.int32)
    table = labels.reshape(top, rows).T
    table = table[jax.random.permutation(jax.random.fold_in(own, 1), rows)]
    rotation = jax.random.randint(jax.random.fold_in(own, 2), (rows, 1), 0, top)
    return jnp.take_along_axis(table, (jnp.arange(top)[None, :] + rotation) % top, axis=1)


def shares(amount, total, limit, skew, full):
    weights = [(1 << 20) // math.isqrt(standing ** skew) + 1 for standing in range(1, amount + 1)]
    largest = limit if full else min(limit, max(-(-total // amount), total * weights[0] // sum(weights)))
    least = 1 if total - largest >= amount - 1 else 0
    given, spare = [largest] + [least] * (amount - 1), total - largest - least * (amount - 1)
    while spare > 0:
        movable = [i for i in range(1, amount) if given[i] < largest] or [i for i in range(1, amount) if given[i] < limit]
        mass, left = sum([weights[i] for i in movable]), spare
        for i in movable:
            extra = min(limit - given[i], max(1, left * weights[i] // mass), spare)
            given[i] = given[i] + extra
            spare = spare - extra
    return np.array(given)


def noise(key, extent, spread, reach, pieces=(), held_as=jnp.bfloat16):
    entries = jax.random.normal(key, extent, jnp.float32) * spread
    if len(pieces) > 0:
        entries = levels(key, extent, pieces, -0.22, 0.18) * entries
    return jnp.clip(entries, min=-reach, max=reach).astype(held_as)


def setup_inputs(seed: int = 0) -> dict:
    seeds = jax.random.split(jax.random.key(seed), 9)
    tokens = noise(seeds[0], (TOKENS, MODEL_DIM), 1.0, 6.0, ((0, 32),))
    token_adapter_index_keys = jax.random.split(jax.random.fold_in(seeds[1], 1), TOKENS // TOK_DEV)
    token_adapter_index_turns = jax.random.permutation(jax.random.fold_in(seeds[1], 3), TOKENS // TOK_DEV)
    token_adapter_index = jax.vmap(lambda own, number: deal_out(jax.random.fold_in(seeds[1], 2), own, number, TOK_DEV, ADAPTER_COUNT, 1, CAP, 2))(token_adapter_index_keys, token_adapter_index_turns).reshape((TOKENS, 1))
    adapter_storage_index = jax.random.permutation(seeds[2], ADAPTER_COUNT).astype(jnp.int32)
    frozen_value_weight = noise(seeds[3], (MODEL_DIM, VALUE_OUT_WIDTH), MODEL_DIM ** -0.5, 0.0625, ((0, 32),))
    frozen_value_bias = noise(seeds[4], (VALUE_OUT_WIDTH,), 0.5, 3.0)
    adapter_down_weight = noise(seeds[5], (ADAPTER_COUNT, MODEL_DIM, ADAPTER_RANK), MODEL_DIM ** -0.5, 0.0625, ((0, 16),))
    adapter_up_weight = noise(seeds[6], (ADAPTER_COUNT, ADAPTER_RANK, VALUE_OUT_WIDTH), ADAPTER_RANK ** -0.5, 0.75, ((0, 16),))
    cotangent = noise(seeds[7], (TOKENS, VALUE_OUT_WIDTH), 0.03125, 0.1875, ((0, 32),))
    return dict(tokens=tokens, token_adapter_index=token_adapter_index, adapter_storage_index=adapter_storage_index, frozen_value_weight=frozen_value_weight, frozen_value_bias=frozen_value_bias, adapter_down_weight=adapter_down_weight, adapter_up_weight=adapter_up_weight, cotangent=cotangent)


def reference(tokens, token_adapter_index, adapter_storage_index, frozen_value_weight, frozen_value_bias, adapter_down_weight, adapter_up_weight, cotangent):
    owner_index = jnp.take(adapter_storage_index, token_adapter_index[:, 0]).astype(jnp.int32)
    onehot = (owner_index[:, None] == jnp.arange(ADAPTER_COUNT, dtype=jnp.int32)[None, :]).astype(jnp.int32)
    place = jnp.sum((jnp.cumsum(onehot, 0).astype(jnp.int32) - onehot) * onehot, 1).astype(jnp.int32)
    longest = CAP * N_FSDP * N_DP
    index_table = jnp.full((ADAPTER_COUNT, longest), TOKENS, jnp.int32)
    index_table = index_table.at[owner_index, place].set(jnp.arange(TOKENS, dtype=jnp.int32))
    token_pad = jnp.concatenate([tokens, jnp.zeros((1, MODEL_DIM), tokens.dtype)], 0)
    cot_pad = jnp.concatenate([cotangent, jnp.zeros((1, VALUE_OUT_WIDTH), cotangent.dtype)], 0)

    def per_adapter(adapter_number):
        picks = index_table[adapter_number]
        token_input_rows = token_pad[picks]
        cotangent_rows = cot_pad[picks]
        rank_activation = jnp.dot(token_input_rows, adapter_down_weight[adapter_number], preferred_element_type=jnp.float32).astype(jnp.bfloat16)
        adapter_delta = jnp.dot(rank_activation, adapter_up_weight[adapter_number], preferred_element_type=jnp.float32).astype(jnp.bfloat16)
        rank_cotangent = jnp.dot(cotangent_rows, adapter_up_weight[adapter_number].T, preferred_element_type=jnp.float32).astype(jnp.bfloat16)
        grad_down = jnp.dot(token_input_rows.T, rank_cotangent, preferred_element_type=jnp.float32)
        grad_up = jnp.dot(rank_activation.T, cotangent_rows, preferred_element_type=jnp.float32)
        return adapter_delta, grad_down, grad_up

    corrections, grad_down, grad_up = lax.map(per_adapter, jnp.arange(ADAPTER_COUNT, dtype=jnp.int32))
    placed = jnp.zeros((TOKENS + 1, VALUE_OUT_WIDTH), corrections.dtype)
    placed = placed.at[index_table.reshape(-1)].set(corrections.reshape(-1, VALUE_OUT_WIDTH))[:TOKENS]
    base_value = jnp.dot(tokens, frozen_value_weight, preferred_element_type=jnp.float32) + frozen_value_bias.astype(jnp.float32)
    values = (base_value + placed.astype(jnp.float32)).astype(jnp.bfloat16)
    return values, grad_down, grad_up
```

```python
import functools

import jax
import jax.numpy as jnp
from jax import lax
from jax.experimental import pallas as pl
from jax.experimental.pallas import tpu as pltpu
from jax.sharding import PartitionSpec as P

MESH = pl.DeviceIdType.MESH
F32 = jnp.float32
BF16 = jnp.bfloat16
PIECES = 4
GROUP = 8


def kernel(
    F, D, NZ,
    tok, de, cot, w, dn, upq, upst, s8, s8t, mask, bias,
    values, gd, gu,
    send, recv, wfull, part, re, ret, back,
    send_sem, recv_sem, wz_send, wz_recv, wp_send, wp_recv, ws_send, ws_recv,
    pt_send, pt_recv, rt_send, rt_recv,
):
    Q = PIECES
    N = F * D
    f, d = lax.axis_index("fsdp"), lax.axis_index("dp")
    me = f * D + d
    z, xy = f // 4, f % 4
    rows, C = send.shape[2], send.shape[3]
    V = cot.shape[1]
    VQ = V // Q
    CQ = C - VQ
    MD = CQ * Q
    R = dn.shape[1] // Q
    capp = rows // Q

    def remote(src, dst, ss, rs, dev):
        return pltpu.make_async_remote_copy(
            src_ref=src, dst_ref=dst, send_sem=ss, recv_sem=rs, device_id=dev, device_id_type=MESH
        )

    barrier = pltpu.get_barrier_semaphore()

    @pl.loop(0, N)
    def _(i):
        @pl.when(i != me)
        def _():
            pl.semaphore_signal(barrier, inc=1, device_id=(i // D, i % D), device_id_type=MESH)

    pl.semaphore_wait(barrier, N - 1)

    own_w = pltpu.make_async_copy(w, wfull.at[z, xy, d], wz_recv.at[0])
    own_w.start()
    z_copies = []
    for k in range(1, NZ):
        to = lax.rem(z + k, NZ)
        z_copies.append(
            remote(w, wfull.at[z, xy, d], wz_send.at[k], wz_recv.at[k], (to * 4 + xy, d))
        )
    for c in z_copies:
        c.start()

    nb = min(256, CQ)
    cot_cat = jnp.concatenate([cot[:, q * VQ:(q + 1) * VQ] for q in range(Q)], 0)
    cot_rows = jnp.dot(de[...], cot_cat, preferred_element_type=F32).astype(BF16)
    cot_rows = cot_rows.reshape(F, rows, VQ)
    for dd in range(D):
        for n in range(CQ // nb):
            piece = jnp.concatenate(
                [tok[:, dd * MD + q * CQ + n * nb:dd * MD + q * CQ + (n + 1) * nb] for q in range(Q)], 0
            )
            out = jnp.dot(de[...], piece, preferred_element_type=F32).astype(BF16)
            send[dd, :, :, n * nb:(n + 1) * nb] = out.reshape(F, rows, nb)
        send[dd, :, :, CQ:] = cot_rows

        @pl.loop(0, F)
        def _(k):
            a = lax.rem(f + k, F)
            is_me = jnp.logical_and(a == f, d == dd)

            @pl.when(is_me)
            def _():
                pltpu.make_async_copy(send.at[dd, a], recv.at[me], recv_sem).start()

            @pl.when(jnp.logical_not(is_me))
            def _():
                remote(send.at[dd, a], recv.at[me], send_sem, recv_sem, (a, dd)).start()

    own_w.wait()
    for c in z_copies:
        c.wait()
    xn, yn = xy + 1 - 2 * (xy % 2), lax.rem(xy + 2, 4)
    line = lambda p: wfull.at[:, p, d]
    p_copies = [
        remote(line(xy), line(xy), wp_send.at[0], wp_recv.at[0], (z * 4 + xn, d)),
        remote(line(xy), line(xy), wp_send.at[1], wp_recv.at[1], (z * 4 + yn, d)),
    ]
    for c in p_copies:
        c.start()
    s_copies = []

    def share(p, slot):
        for k in range(1, D):
            c = remote(
                line(p), line(p), ws_send.at[slot, k], ws_recv.at[slot, k], (f, lax.rem(d + k, D))
            )
            c.start()
            s_copies.append(c)

    share(xy, 0)
    half = NZ // 2
    top = lambda p: wfull.at[0:half, p, d]
    low_half = lambda p: wfull.at[half:NZ, p, d]
    p_copies[0].wait()
    c2 = remote(top(xn), top(xn), wp_send.at[2], wp_recv.at[2], (z * 4 + yn, d))
    c2.start()
    share(xn, 1)
    p_copies[1].wait()
    c3 = remote(low_half(yn), low_half(yn), wp_send.at[3], wp_recv.at[3], (z * 4 + xn, d))
    c3.start()
    share(yn, 2)
    c2.wait()
    c3.wait()
    share(3 - xy, 3)
    for c in s_copies:
        c.wait()

    total = jnp.broadcast_to(bias[...].astype(F32), (tok.shape[0], V))
    M = tok.shape[1]
    steps = NZ
    kk = M // steps
    for i in range(steps):
        block = wfull[i].reshape(kk, V)
        total = total + jnp.dot(tok[:, i * kk:(i + 1) * kk], block, preferred_element_type=F32)

    pltpu.make_async_copy(recv, recv, recv_sem).wait()
    G = GROUP
    gr, gc = G * rows, G * capp

    def gather_rows(x):
        x = x * mask[...]
        hi = x.astype(BF16)
        r1 = x - hi.astype(F32)
        mid = r1.astype(BF16)
        lo = (r1 - mid.astype(F32)).astype(BF16)
        y = jnp.dot(s8[...], hi, preferred_element_type=F32)
        y = y + jnp.dot(s8[...], mid, preferred_element_type=F32)
        y = y + jnp.dot(s8[...], lo, preferred_element_type=F32)
        return sum([y[:, q * R:(q + 1) * R] for q in range(Q)])

    def spread_rows(x):
        x = jnp.concatenate([x] * Q, 1)
        return (jnp.dot(s8t[...], x, preferred_element_type=F32) * mask[...]).astype(BF16)

    @pl.loop(0, N // G)
    def _(g):
        x = recv[pl.ds(g * G, G), :, 0:CQ].reshape(gr, CQ)
        p = gather_rows(jnp.dot(x, dn[...], preferred_element_type=F32))
        part[d, pl.ds(pl.multiple_of(g * gc, 8), gc), :] = jnp.concatenate([p] * (128 // R), 1)
        c = recv[pl.ds(g * G, G), :, CQ:C].reshape(gr, VQ)
        rc = gather_rows(jnp.dot(c, upq[...], preferred_element_type=F32)).astype(BF16)
        re[g] = spread_rows(rc)

    pt_copies = [
        remote(part.at[d], part.at[d], pt_send.at[k], pt_recv.at[k], (f, lax.rem(d + k, D)))
        for k in range(1, D)
    ]
    for c in pt_copies:
        c.start()
    for c in pt_copies:
        c.wait()
    gu[...] = jnp.zeros_like(gu)

    @pl.loop(0, N // G)
    def _(g):
        at = pl.ds(pl.multiple_of(g * gc, 8), gc)
        low = sum([part[k, at, 0:R] for k in range(D)]).astype(BF16)
        le = spread_rows(low)
        ret[pl.ds(g * G, G)] = (
            jnp.dot(le, upst[...], preferred_element_type=F32).astype(BF16).reshape(G, rows, VQ)
        )
        c = recv[pl.ds(g * G, G), :, CQ:C].reshape(gr, VQ)
        gu[...] += lax.dot_general(le, c, (((0,), (0,)), ((), ())), preferred_element_type=F32)

    @pl.loop(0, F)
    def _(k):
        s = lax.rem(f + k, F)

        @pl.when(s == f)
        def _():
            pltpu.make_async_copy(ret.at[s * D + d], back.at[f], rt_recv).start()

        @pl.when(s != f)
        def _():
            remote(ret.at[s * D + d], back.at[f], rt_send, rt_recv, (s, d)).start()

    gd[...] = jnp.zeros_like(gd)

    @pl.loop(0, N // G)
    def _(g):
        x = recv[pl.ds(g * G, G), :, 0:CQ].reshape(gr, CQ)
        gd[...] += lax.dot_general(x, re[g], (((0,), (0,)), ((), ())), preferred_element_type=F32)

    pltpu.make_async_copy(back, back, rt_recv).wait()
    T = tok.shape[0]
    b = back[...].reshape(F * rows, VQ)
    placed = lax.dot_general(de[...], b, (((0,), (0,)), ((), ())), preferred_element_type=F32)
    placed = jnp.concatenate([placed[q * T:(q + 1) * T] for q in range(Q)], 1)
    values[...] = (total + placed).astype(BF16)

    pltpu.make_async_copy(recv.at[0:N - 1], recv.at[0:N - 1], send_sem).wait()
    pltpu.make_async_copy(back.at[0:F - 1], back.at[0:F - 1], rt_send).wait()


def body(tokens, token_adapter_index, adapter_storage_index, weight, bias, down, up, cotangent):
    F, D = lax.axis_size("fsdp"), lax.axis_size("dp")
    T, M = tokens.shape
    V = weight.shape[1]
    A = adapter_storage_index.shape[0]
    R = down.shape[2]
    Q = PIECES
    N = F * D
    cap = max(2, (3 * T + 2 * F - 1) // (2 * F))
    capp = -(-cap // Q) * Q
    rows = Q * capp
    MD, VQ = M // D, V // Q
    CQ = MD // Q
    NZ = F // 4
    d = lax.axis_index("dp")

    hot = token_adapter_index == jnp.arange(A)[None, :]
    owner = jnp.sum(jnp.where(hot, adapter_storage_index[None, :], 0), 1)
    i = jnp.arange(T)
    same = (owner[:, None] == owner[None, :]) & (i[None, :] < i[:, None])
    target = owner * capp + jnp.sum(same.astype(jnp.int32), 1)
    code = jnp.arange(A)[:, None, None] * capp + jnp.arange(capp)[None, None, :]
    code = jnp.broadcast_to(code, (A, Q, capp)).reshape(A * rows, 1, 1)
    q_row = jnp.broadcast_to(jnp.arange(Q)[None, :, None], (A, Q, capp)).reshape(A * rows, 1, 1)
    de = (code == target[None, None, :]) & (q_row == jnp.arange(Q)[None, :, None])
    de = de.astype(BF16).reshape(A * rows, Q * T)

    mine = lax.dynamic_slice_in_dim(down[0], d * MD, MD, 0)
    dn = mine.reshape(Q, CQ, R).transpose(1, 0, 2).reshape(CQ, Q * R)
    upst = up[0].reshape(R, Q, VQ).transpose(1, 0, 2).reshape(Q * R, VQ)
    upq = upst.T

    gr, gc = GROUP * rows, GROUP * capp
    rr, cc = jnp.arange(gr), jnp.arange(gc)
    from_row = (rr // rows) * capp + rr % capp
    s8t = (from_row[:, None] == cc[None, :]).astype(BF16)
    s8 = s8t.T
    mask = (((rr % rows) // capp)[:, None] == (jnp.arange(Q * R) // R)[None, :]).astype(F32)

    vmem = pl.BlockSpec(memory_space=pltpu.VMEM)
    dma = pltpu.SemaphoreType.DMA
    values, gd, gu = pl.pallas_call(
        functools.partial(kernel, F, D, NZ),
        out_shape=(
            jax.ShapeDtypeStruct((T, V), BF16),
            jax.ShapeDtypeStruct((CQ, Q * R), F32),
            jax.ShapeDtypeStruct((Q * R, VQ), F32),
        ),
        in_specs=[vmem] * 11,
        out_specs=(vmem,) * 3,
        scratch_shapes=[
            pltpu.VMEM((D, F, rows, CQ + VQ), BF16),
            pltpu.VMEM((N, rows, CQ + VQ), BF16),
            pltpu.VMEM((NZ, 4, D, M // N, V), BF16),
            pltpu.VMEM((D, N * capp, 128), F32),
            pltpu.VMEM((N // GROUP, gr, Q * R), BF16),
            pltpu.VMEM((N, rows, VQ), BF16),
            pltpu.VMEM((F, rows, VQ), BF16),
            dma, dma,
            dma((NZ,)), dma((NZ,)),
            dma((4,)), dma((4,)),
            dma((4, D)), dma((4, D)),
            dma((D,)), dma((D,)),
            dma, dma,
        ],
        compiler_params=pltpu.CompilerParams(
            collective_id=0, has_side_effects=True, vmem_limit_bytes=56 * 2**20
        ),
    )(tokens, de, cotangent, weight, dn, upq, upst, s8, s8t, mask, bias[None, :])
    gd = gd.reshape(CQ, Q, R).transpose(1, 0, 2).reshape(1, MD, R)
    gu = gu.reshape(Q, R, VQ).transpose(1, 0, 2).reshape(R, V)
    gu = lax.dynamic_slice_in_dim(gu, d * (V // D), V // D, 1)[None]
    return values, gd, gu


def solution(mesh):
    return jax.shard_map(
        body,
        mesh=mesh,
        in_specs=(
            P(("fsdp", "dp"), None),
            P(("fsdp", "dp"), None),
            P(),
            P(("fsdp", "dp"), None),
            P(),
            P("fsdp", None, None),
            P("fsdp", None, None),
            P(("fsdp", "dp"), None),
        ),
        out_specs=(P(("fsdp", "dp"), None), P("fsdp", "dp", None), P("fsdp", None, "dp")),
        check_vma=False,
    )
```

```python
import functools

import jax
import jax.numpy as jnp
import numpy as np
from jax import lax
from jax.experimental import pallas as pl
from jax.experimental.pallas import tpu as pltpu
from jax.sharding import PartitionSpec as P

MESH = pl.DeviceIdType.MESH
F32 = jnp.float32
BF16 = jnp.bfloat16
PIECES = 4
GROUP = 8


def kernel(
    F, D, NZ,
    tok, de, cot, w, dn, upq, upst, s8, s8t, mask, bias,
    values, gd, gu,
    send, recv, wfull, part, re, ret, back,
    send_sem, recv_sem, wz_send, wz_recv, wp_send, wp_recv, ws_send, ws_recv,
    pt_send, pt_recv, rt_send, rt_recv,
):
    Q = PIECES
    N = F * D
    f, d = lax.axis_index("fsdp"), lax.axis_index("dp")
    me = f * D + d
    z, xy = f // 4, f % 4
    rows, C = send.shape[2], send.shape[3]
    V = cot.shape[1]
    VQ = V // Q
    CQ = C - VQ
    MD = CQ * Q
    R = dn.shape[1] // Q
    capp = rows // Q

    def remote(src, dst, ss, rs, dev):
        return pltpu.make_async_remote_copy(
            src_ref=src, dst_ref=dst, send_sem=ss, recv_sem=rs, device_id=dev, device_id_type=MESH
        )

    barrier = pltpu.get_barrier_semaphore()

    @pl.loop(0, N)
    def _(i):
        @pl.when(i != me)
        def _():
            pl.semaphore_signal(barrier, inc=1, device_id=(i // D, i % D), device_id_type=MESH)

    pl.semaphore_wait(barrier, N - 1)

    own_w = pltpu.make_async_copy(w, wfull.at[z, xy, d], wz_recv.at[0])
    own_w.start()
    z_copies = []
    for k in range(1, NZ):
        to = lax.rem(z + k, NZ)
        z_copies.append(
            remote(w, wfull.at[z, xy, d], wz_send.at[k], wz_recv.at[k], (to * 4 + xy, d))
        )
    for c in z_copies:
        c.start()

    nb = min(256, CQ)
    cot_cat = jnp.concatenate([cot[:, q * VQ:(q + 1) * VQ] for q in range(Q)], 0)
    cot_rows = jnp.dot(de[...], cot_cat, preferred_element_type=F32).astype(BF16)
    cot_rows = cot_rows.reshape(F, rows, VQ)
    for dd in range(D):
        for n in range(CQ // nb):
            piece = jnp.concatenate(
                [tok[:, dd * MD + q * CQ + n * nb:dd * MD + q * CQ + (n + 1) * nb] for q in range(Q)], 0
            )
            out = jnp.dot(de[...], piece, preferred_element_type=F32).astype(BF16)
            send[dd, :, :, n * nb:(n + 1) * nb] = out.reshape(F, rows, nb)
        send[dd, :, :, CQ:] = cot_rows

        @pl.loop(0, F)
        def _(k):
            a = lax.rem(f + k, F)
            is_me = jnp.logical_and(a == f, d == dd)

            @pl.when(is_me)
            def _():
                pltpu.make_async_copy(send.at[dd, a], recv.at[me], recv_sem).start()

            @pl.when(jnp.logical_not(is_me))
            def _():
                remote(send.at[dd, a], recv.at[me], send_sem, recv_sem, (a, dd)).start()

    own_w.wait()
    for c in z_copies:
        c.wait()
    xn, yn = xy + 1 - 2 * (xy % 2), lax.rem(xy + 2, 4)
    line = lambda p: wfull.at[:, p, d]
    p_copies = [
        remote(line(xy), line(xy), wp_send.at[0], wp_recv.at[0], (z * 4 + xn, d)),
        remote(line(xy), line(xy), wp_send.at[1], wp_recv.at[1], (z * 4 + yn, d)),
    ]
    for c in p_copies:
        c.start()
    s_copies = []

    def share(p, slot):
        for k in range(1, D):
            c = remote(
                line(p), line(p), ws_send.at[slot, k], ws_recv.at[slot, k], (f, lax.rem(d + k, D))
            )
            c.start()
            s_copies.append(c)

    share(xy, 0)
    half = NZ // 2
    top = lambda p: wfull.at[0:half, p, d]
    low_half = lambda p: wfull.at[half:NZ, p, d]
    p_copies[0].wait()
    c2 = remote(top(xn), top(xn), wp_send.at[2], wp_recv.at[2], (z * 4 + yn, d))
    c2.start()
    share(xn, 1)
    p_copies[1].wait()
    c3 = remote(low_half(yn), low_half(yn), wp_send.at[3], wp_recv.at[3], (z * 4 + xn, d))
    c3.start()
    share(yn, 2)

    pltpu.make_async_copy(recv, recv, recv_sem).wait()
    G = GROUP
    gr, gc = G * rows, G * capp

    def gather_rows(x):
        x = x * mask[...]
        hi = x.astype(BF16)
        r1 = x - hi.astype(F32)
        mid = r1.astype(BF16)
        lo = (r1 - mid.astype(F32)).astype(BF16)
        y = jnp.dot(s8[...], hi, preferred_element_type=F32)
        y = y + jnp.dot(s8[...], mid, preferred_element_type=F32)
        y = y + jnp.dot(s8[...], lo, preferred_element_type=F32)
        return sum([y[:, q * R:(q + 1) * R] for q in range(Q)])

    def spread_rows(x):
        x = jnp.concatenate([x] * Q, 1)
        return (jnp.dot(s8t[...], x, preferred_element_type=F32) * mask[...]).astype(BF16)

    @pl.loop(0, N // G)
    def _(g):
        x = recv[pl.ds(g * G, G), :, 0:CQ].reshape(gr, CQ)
        p = gather_rows(jnp.dot(x, dn[...], preferred_element_type=F32))
        part[d, pl.ds(pl.multiple_of(g * gc, 8), gc), :] = jnp.concatenate([p] * (128 // R), 1)
        c = recv[pl.ds(g * G, G), :, CQ:C].reshape(gr, VQ)
        rc = gather_rows(jnp.dot(c, upq[...], preferred_element_type=F32)).astype(BF16)
        re[g] = spread_rows(rc)

    pt_copies = [
        remote(part.at[d], part.at[d], pt_send.at[k], pt_recv.at[k], (f, lax.rem(d + k, D)))
        for k in range(1, D)
    ]
    for c in pt_copies:
        c.start()
    for c in pt_copies:
        c.wait()
    gu[...] = jnp.zeros_like(gu)

    @pl.loop(0, N // G)
    def _(g):
        at = pl.ds(pl.multiple_of(g * gc, 8), gc)
        low = sum([part[k, at, 0:R] for k in range(D)]).astype(BF16)
        le = spread_rows(low)
        ret[pl.ds(g * G, G)] = (
            jnp.dot(le, upst[...], preferred_element_type=F32).astype(BF16).reshape(G, rows, VQ)
        )
        c = recv[pl.ds(g * G, G), :, CQ:C].reshape(gr, VQ)
        gu[...] += lax.dot_general(le, c, (((0,), (0,)), ((), ())), preferred_element_type=F32)

    @pl.loop(0, F)
    def _(k):
        s = lax.rem(f + k, F)

        @pl.when(s == f)
        def _():
            pltpu.make_async_copy(ret.at[s * D + d], back.at[f], rt_recv).start()

        @pl.when(s != f)
        def _():
            remote(ret.at[s * D + d], back.at[f], rt_send, rt_recv, (s, d)).start()

    c2.wait()
    c3.wait()
    share(3 - xy, 3)

    gd[...] = jnp.zeros_like(gd)

    @pl.loop(0, N // G)
    def _(g):
        x = recv[pl.ds(g * G, G), :, 0:CQ].reshape(gr, CQ)
        gd[...] += lax.dot_general(x, re[g], (((0,), (0,)), ((), ())), preferred_element_type=F32)

    for c in s_copies:
        c.wait()

    total = jnp.broadcast_to(bias[...].astype(F32), (tok.shape[0], V))
    M = tok.shape[1]
    steps = NZ
    kk = M // steps
    for i in range(steps):
        block = wfull[i].reshape(kk, V)
        total = total + jnp.dot(tok[:, i * kk:(i + 1) * kk], block, preferred_element_type=F32)

    pltpu.make_async_copy(back, back, rt_recv).wait()
    T = tok.shape[0]
    b = back[...].reshape(F * rows, VQ)
    placed = lax.dot_general(de[...], b, (((0,), (0,)), ((), ())), preferred_element_type=F32)
    placed = jnp.concatenate([placed[q * T:(q + 1) * T] for q in range(Q)], 1)
    values[...] = (total + placed).astype(BF16)

    pltpu.make_async_copy(recv.at[0:N - 1], recv.at[0:N - 1], send_sem).wait()
    pltpu.make_async_copy(back.at[0:F - 1], back.at[0:F - 1], rt_send).wait()


def body(tokens, token_adapter_index, adapter_storage_index, weight, bias, down, up, cotangent):
    F, D = lax.axis_size("fsdp"), lax.axis_size("dp")
    T, M = tokens.shape
    V = weight.shape[1]
    A = adapter_storage_index.shape[0]
    R = down.shape[2]
    Q = PIECES
    N = F * D
    cap = max(2, (3 * T + 2 * F - 1) // (2 * F))
    capp = -(-cap // Q) * Q
    rows = Q * capp
    MD, VQ = M // D, V // Q
    CQ = MD // Q
    NZ = F // 4
    d = lax.axis_index("dp")

    hot = token_adapter_index == jnp.arange(A)[None, :]
    owner = jnp.sum(jnp.where(hot, adapter_storage_index[None, :], 0), 1)
    i = jnp.arange(T)
    same = (owner[:, None] == owner[None, :]) & (i[None, :] < i[:, None])
    target = owner * capp + jnp.sum(same.astype(jnp.int32), 1)
    code = jnp.arange(A)[:, None, None] * capp + jnp.arange(capp)[None, None, :]
    code = jnp.broadcast_to(code, (A, Q, capp)).reshape(A * rows, 1, 1)
    q_row = jnp.broadcast_to(jnp.arange(Q)[None, :, None], (A, Q, capp)).reshape(A * rows, 1, 1)
    de = (code == target[None, None, :]) & (q_row == jnp.arange(Q)[None, :, None])
    de = de.astype(BF16).reshape(A * rows, Q * T)

    mine = lax.dynamic_slice_in_dim(down[0], d * MD, MD, 0)
    dn = mine.reshape(Q, CQ, R).transpose(1, 0, 2).reshape(CQ, Q * R)
    upst = up[0].reshape(R, Q, VQ).transpose(1, 0, 2).reshape(Q * R, VQ)
    upq = upst.T

    gr, gc = GROUP * rows, GROUP * capp
    rr, cc = np.arange(gr), np.arange(gc)
    from_row = (rr // rows) * capp + rr % capp
    s8t = (from_row[:, None] == cc[None, :]).astype(BF16)
    s8 = s8t.T
    mask = (((rr % rows) // capp)[:, None] == (np.arange(Q * R) // R)[None, :]).astype(np.float32)

    vmem = pl.BlockSpec(memory_space=pltpu.VMEM)
    dma = pltpu.SemaphoreType.DMA
    values, gd, gu = pl.pallas_call(
        functools.partial(kernel, F, D, NZ),
        out_shape=(
            jax.ShapeDtypeStruct((T, V), BF16),
            jax.ShapeDtypeStruct((CQ, Q * R), F32),
            jax.ShapeDtypeStruct((Q * R, VQ), F32),
        ),
        in_specs=[vmem] * 11,
        out_specs=(vmem,) * 3,
        scratch_shapes=[
            pltpu.VMEM((D, F, rows, CQ + VQ), BF16),
            pltpu.VMEM((N, rows, CQ + VQ), BF16),
            pltpu.VMEM((NZ, 4, D, M // N, V), BF16),
            pltpu.VMEM((D, N * capp, 128), F32),
            pltpu.VMEM((N // GROUP, gr, Q * R), BF16),
            pltpu.VMEM((N, rows, VQ), BF16),
            pltpu.VMEM((F, rows, VQ), BF16),
            dma, dma,
            dma((NZ,)), dma((NZ,)),
            dma((4,)), dma((4,)),
            dma((4, D)), dma((4, D)),
            dma((D,)), dma((D,)),
            dma, dma,
        ],
        compiler_params=pltpu.CompilerParams(
            collective_id=0, has_side_effects=True, vmem_limit_bytes=56 * 2**20
        ),
    )(tokens, de, cotangent, weight, dn, upq, upst, s8, s8t, mask, bias[None, :])
    gd = gd.reshape(CQ, Q, R).transpose(1, 0, 2).reshape(1, MD, R)
    gu = gu.reshape(Q, R, VQ).transpose(1, 0, 2).reshape(R, V)
    gu = lax.dynamic_slice_in_dim(gu, d * (V // D), V // D, 1)[None]
    return values, gd, gu


def solution(mesh):
    return jax.shard_map(
        body,
        mesh=mesh,
        in_specs=(
            P(("fsdp", "dp"), None),
            P(("fsdp", "dp"), None),
            P(),
            P(("fsdp", "dp"), None),
            P(),
            P("fsdp", None, None),
            P("fsdp", None, None),
            P(("fsdp", "dp"), None),
        ),
        out_specs=(P(("fsdp", "dp"), None), P("fsdp", "dp", None), P("fsdp", None, "dp")),
        check_vma=False,
    )
```

```python
import functools

import jax
import jax.numpy as jnp
import numpy as np
from jax import lax
from jax.experimental import pallas as pl
from jax.experimental.pallas import tpu as pltpu
from jax.sharding import PartitionSpec as P

MESH = pl.DeviceIdType.MESH
F32 = jnp.float32
BF16 = jnp.bfloat16
PIECES = 4
GROUP = 8


def kernel(
    F, D, NZ,
    tok, de, cot, w, dn, upq, upst, s8, s8t, mask, bias,
    values, gd, gu,
    send, recv, wfull, part, re, ret, back,
    send_sem, recv_sem, wz_send, wz_recv, wp_send, wp_recv, ws_send, ws_recv,
    pt_send, pt_recv, rt_send, rt_recv,
):
    Q = PIECES
    N = F * D
    f, d = lax.axis_index("fsdp"), lax.axis_index("dp")
    me = f * D + d
    z, xy = f // 4, f % 4
    rows, C = send.shape[2], send.shape[3]
    V = cot.shape[1]
    VQ = V // Q
    CQ = C - VQ
    MD = CQ * Q
    R = dn.shape[1] // Q
    capp = rows // Q

    def remote(src, dst, ss, rs, dev):
        return pltpu.make_async_remote_copy(
            src_ref=src, dst_ref=dst, send_sem=ss, recv_sem=rs, device_id=dev, device_id_type=MESH
        )

    barrier = pltpu.get_barrier_semaphore()

    @pl.loop(0, N)
    def _(i):
        @pl.when(i != me)
        def _():
            pl.semaphore_signal(barrier, inc=1, device_id=(i // D, i % D), device_id_type=MESH)

    pl.semaphore_wait(barrier, N - 1)

    own_w = pltpu.make_async_copy(w, wfull.at[z, xy, d], wz_recv.at[0])
    own_w.start()
    z_copies = []
    for k in range(1, NZ):
        to = lax.rem(z + k, NZ)
        z_copies.append(
            remote(w, wfull.at[z, xy, d], wz_send.at[k], wz_recv.at[k], (to * 4 + xy, d))
        )
    for c in z_copies:
        c.start()

    nb = min(256, CQ)
    cot_cat = jnp.concatenate([cot[:, q * VQ:(q + 1) * VQ] for q in range(Q)], 0)
    cot_rows = jnp.dot(de[...], cot_cat, preferred_element_type=F32).astype(BF16)
    cot_rows = cot_rows.reshape(F, rows, VQ)
    for dd in range(D):
        for n in range(CQ // nb):
            piece = jnp.concatenate(
                [tok[:, dd * MD + q * CQ + n * nb:dd * MD + q * CQ + (n + 1) * nb] for q in range(Q)], 0
            )
            out = jnp.dot(de[...], piece, preferred_element_type=F32).astype(BF16)
            send[dd, :, :, n * nb:(n + 1) * nb] = out.reshape(F, rows, nb)
        send[dd, :, :, CQ:] = cot_rows

        @pl.loop(0, F)
        def _(k):
            a = lax.rem(f + F // 2 + k, F)
            is_me = jnp.logical_and(a == f, d == dd)

            @pl.when(is_me)
            def _():
                pltpu.make_async_copy(send.at[dd, a], recv.at[me], recv_sem).start()

            @pl.when(jnp.logical_not(is_me))
            def _():
                remote(send.at[dd, a], recv.at[me], send_sem, recv_sem, (a, dd)).start()

    own_w.wait()
    for c in z_copies:
        c.wait()
    xn, yn = xy + 1 - 2 * (xy % 2), lax.rem(xy + 2, 4)
    line = lambda p: wfull.at[:, p, d]
    p_copies = [
        remote(line(xy), line(xy), wp_send.at[0], wp_recv.at[0], (z * 4 + xn, d)),
        remote(line(xy), line(xy), wp_send.at[1], wp_recv.at[1], (z * 4 + yn, d)),
    ]
    for c in p_copies:
        c.start()
    s_copies = []

    def share(p, slot):
        for k in range(1, D):
            c = remote(
                line(p), line(p), ws_send.at[slot, k], ws_recv.at[slot, k], (f, lax.rem(d + k, D))
            )
            c.start()
            s_copies.append(c)

    share(xy, 0)
    half = NZ // 2
    top = lambda p: wfull.at[0:half, p, d]
    low_half = lambda p: wfull.at[half:NZ, p, d]
    p_copies[0].wait()
    c2 = remote(top(xn), top(xn), wp_send.at[2], wp_recv.at[2], (z * 4 + yn, d))
    c2.start()
    share(xn, 1)
    p_copies[1].wait()
    c3 = remote(low_half(yn), low_half(yn), wp_send.at[3], wp_recv.at[3], (z * 4 + xn, d))
    c3.start()
    share(yn, 2)

    pltpu.make_async_copy(recv, recv, recv_sem).wait()
    G = GROUP
    gr, gc = G * rows, G * capp

    def gather_rows(x):
        x = x * mask[...]
        hi = x.astype(BF16)
        r1 = x - hi.astype(F32)
        mid = r1.astype(BF16)
        lo = (r1 - mid.astype(F32)).astype(BF16)
        y = jnp.dot(s8[...], hi, preferred_element_type=F32)
        y = y + jnp.dot(s8[...], mid, preferred_element_type=F32)
        y = y + jnp.dot(s8[...], lo, preferred_element_type=F32)
        return sum([y[:, q * R:(q + 1) * R] for q in range(Q)])

    def spread_rows(x):
        x = jnp.concatenate([x] * Q, 1)
        return (jnp.dot(s8t[...], x, preferred_element_type=F32) * mask[...]).astype(BF16)

    @pl.loop(0, N // G)
    def _(g):
        x = recv[pl.ds(g * G, G), :, 0:CQ].reshape(gr, CQ)
        p = gather_rows(jnp.dot(x, dn[...], preferred_element_type=F32))
        part[d, pl.ds(pl.multiple_of(g * gc, 8), gc), :] = jnp.concatenate([p] * (128 // R), 1)
        c = recv[pl.ds(g * G, G), :, CQ:C].reshape(gr, VQ)
        rc = gather_rows(jnp.dot(c, upq[...], preferred_element_type=F32)).astype(BF16)
        re[g] = spread_rows(rc)

    pt_copies = [
        remote(part.at[d], part.at[d], pt_send.at[k], pt_recv.at[k], (f, lax.rem(d + k, D)))
        for k in range(1, D)
    ]
    for c in pt_copies:
        c.start()
    for c in pt_copies:
        c.wait()
    gu[...] = jnp.zeros_like(gu)

    @pl.loop(0, N // G)
    def _(g):
        at = pl.ds(pl.multiple_of(g * gc, 8), gc)
        low = sum([part[k, at, 0:R] for k in range(D)]).astype(BF16)
        le = spread_rows(low)
        ret[pl.ds(g * G, G)] = (
            jnp.dot(le, upst[...], preferred_element_type=F32).astype(BF16).reshape(G, rows, VQ)
        )
        c = recv[pl.ds(g * G, G), :, CQ:C].reshape(gr, VQ)
        gu[...] += lax.dot_general(le, c, (((0,), (0,)), ((), ())), preferred_element_type=F32)

    @pl.loop(0, F)
    def _(k):
        s = lax.rem(f + k, F)

        @pl.when(s == f)
        def _():
            pltpu.make_async_copy(ret.at[s * D + d], back.at[f], rt_recv).start()

        @pl.when(s != f)
        def _():
            remote(ret.at[s * D + d], back.at[f], rt_send, rt_recv, (s, d)).start()

    c2.wait()
    c3.wait()
    share(3 - xy, 3)

    gd[...] = jnp.zeros_like(gd)

    @pl.loop(0, N // G)
    def _(g):
        x = recv[pl.ds(g * G, G), :, 0:CQ].reshape(gr, CQ)
        gd[...] += lax.dot_general(x, re[g], (((0,), (0,)), ((), ())), preferred_element_type=F32)

    for c in s_copies:
        c.wait()

    total = jnp.broadcast_to(bias[...].astype(F32), (tok.shape[0], V))
    M = tok.shape[1]
    steps = NZ
    kk = M // steps
    for i in range(steps):
        block = wfull[i].reshape(kk, V)
        total = total + jnp.dot(tok[:, i * kk:(i + 1) * kk], block, preferred_element_type=F32)

    pltpu.make_async_copy(back, back, rt_recv).wait()
    T = tok.shape[0]
    b = back[...].reshape(F * rows, VQ)
    placed = lax.dot_general(de[...], b, (((0,), (0,)), ((), ())), preferred_element_type=F32)
    placed = jnp.concatenate([placed[q * T:(q + 1) * T] for q in range(Q)], 1)
    values[...] = (total + placed).astype(BF16)

    pltpu.make_async_copy(recv.at[0:N - 1], recv.at[0:N - 1], send_sem).wait()
    pltpu.make_async_copy(back.at[0:F - 1], back.at[0:F - 1], rt_send).wait()


def body(tokens, token_adapter_index, adapter_storage_index, weight, bias, down, up, cotangent):
    F, D = lax.axis_size("fsdp"), lax.axis_size("dp")
    T, M = tokens.shape
    V = weight.shape[1]
    A = adapter_storage_index.shape[0]
    R = down.shape[2]
    Q = PIECES
    N = F * D
    cap = max(2, (3 * T + 2 * F - 1) // (2 * F))
    capp = -(-cap // Q) * Q
    rows = Q * capp
    MD, VQ = M // D, V // Q
    CQ = MD // Q
    NZ = F // 4
    d = lax.axis_index("dp")

    hot = token_adapter_index == jnp.arange(A)[None, :]
    owner = jnp.sum(jnp.where(hot, adapter_storage_index[None, :], 0), 1)
    i = jnp.arange(T)
    same = (owner[:, None] == owner[None, :]) & (i[None, :] < i[:, None])
    target = owner * capp + jnp.sum(same.astype(jnp.int32), 1)
    code = jnp.arange(A)[:, None, None] * capp + jnp.arange(capp)[None, None, :]
    code = jnp.broadcast_to(code, (A, Q, capp)).reshape(A * rows, 1, 1)
    q_row = jnp.broadcast_to(jnp.arange(Q)[None, :, None], (A, Q, capp)).reshape(A * rows, 1, 1)
    de = (code == target[None, None, :]) & (q_row == jnp.arange(Q)[None, :, None])
    de = de.astype(BF16).reshape(A * rows, Q * T)

    mine = lax.dynamic_slice_in_dim(down[0], d * MD, MD, 0)
    dn = mine.reshape(Q, CQ, R).transpose(1, 0, 2).reshape(CQ, Q * R)
    upst = up[0].reshape(R, Q, VQ).transpose(1, 0, 2).reshape(Q * R, VQ)
    upq = upst.T

    gr, gc = GROUP * rows, GROUP * capp
    rr, cc = np.arange(gr), np.arange(gc)
    from_row = (rr // rows) * capp + rr % capp
    s8t = (from_row[:, None] == cc[None, :]).astype(BF16)
    s8 = s8t.T
    mask = (((rr % rows) // capp)[:, None] == (np.arange(Q * R) // R)[None, :]).astype(np.float32)

    vmem = pl.BlockSpec(memory_space=pltpu.VMEM)
    dma = pltpu.SemaphoreType.DMA
    values, gd, gu = pl.pallas_call(
        functools.partial(kernel, F, D, NZ),
        out_shape=(
            jax.ShapeDtypeStruct((T, V), BF16),
            jax.ShapeDtypeStruct((CQ, Q * R), F32),
            jax.ShapeDtypeStruct((Q * R, VQ), F32),
        ),
        in_specs=[vmem] * 11,
        out_specs=(vmem,) * 3,
        scratch_shapes=[
            pltpu.VMEM((D, F, rows, CQ + VQ), BF16),
            pltpu.VMEM((N, rows, CQ + VQ), BF16),
            pltpu.VMEM((NZ, 4, D, M // N, V), BF16),
            pltpu.VMEM((D, N * capp, 128), F32),
            pltpu.VMEM((N // GROUP, gr, Q * R), BF16),
            pltpu.VMEM((N, rows, VQ), BF16),
            pltpu.VMEM((F, rows, VQ), BF16),
            dma, dma,
            dma((NZ,)), dma((NZ,)),
            dma((4,)), dma((4,)),
            dma((4, D)), dma((4, D)),
            dma((D,)), dma((D,)),
            dma, dma,
        ],
        compiler_params=pltpu.CompilerParams(
            collective_id=0, has_side_effects=True, vmem_limit_bytes=56 * 2**20
        ),
    )(tokens, de, cotangent, weight, dn, upq, upst, s8, s8t, mask, bias[None, :])
    gd = gd.reshape(CQ, Q, R).transpose(1, 0, 2).reshape(1, MD, R)
    gu = gu.reshape(Q, R, VQ).transpose(1, 0, 2).reshape(R, V)
    gu = lax.dynamic_slice_in_dim(gu, d * (V // D), V // D, 1)[None]
    return values, gd, gu


def solution(mesh):
    return jax.shard_map(
        body,
        mesh=mesh,
        in_specs=(
            P(("fsdp", "dp"), None),
            P(("fsdp", "dp"), None),
            P(),
            P(("fsdp", "dp"), None),
            P(),
            P("fsdp", None, None),
            P("fsdp", None, None),
            P(("fsdp", "dp"), None),
        ),
        out_specs=(P(("fsdp", "dp"), None), P("fsdp", "dp", None), P("fsdp", None, "dp")),
        check_vma=False,
    )
```

```python
import functools

import jax
import jax.numpy as jnp
import numpy as np
from jax import lax
from jax.experimental import pallas as pl
from jax.experimental.pallas import tpu as pltpu
from jax.sharding import PartitionSpec as P

MESH = pl.DeviceIdType.MESH
F32 = jnp.float32
BF16 = jnp.bfloat16
PIECES = 4
GROUP = 8


def kernel(
    F, D, NZ,
    tok, de, cot, w, dn, upq, upst, s8, s8t, mask, bias,
    values, gd, gu,
    send, recv, wfull, part, re, ret, back,
    send_sem, recv_sem, wz_send, wz_recv, wp_send, wp_recv, ws_send, ws_recv,
    pt_send, pt_recv, rt_send, rt_recv,
):
    Q = PIECES
    N = F * D
    f, d = lax.axis_index("fsdp"), lax.axis_index("dp")
    me = f * D + d
    z, xy = f // 4, f % 4
    rows, C = send.shape[2], send.shape[3]
    V = cot.shape[1]
    VQ = V // Q
    CQ = C - VQ
    MD = CQ * Q
    R = dn.shape[1] // Q
    capp = rows // Q

    def remote(src, dst, ss, rs, dev):
        return pltpu.make_async_remote_copy(
            src_ref=src, dst_ref=dst, send_sem=ss, recv_sem=rs, device_id=dev, device_id_type=MESH
        )

    barrier = pltpu.get_barrier_semaphore()

    @pl.loop(0, N)
    def _(i):
        @pl.when(i != me)
        def _():
            pl.semaphore_signal(barrier, inc=1, device_id=(i // D, i % D), device_id_type=MESH)

    pl.semaphore_wait(barrier, N - 1)

    own_w = pltpu.make_async_copy(w, wfull.at[z, xy, d], wz_recv.at[0])
    own_w.start()
    z_copies = []
    for k in range(1, NZ):
        to = lax.rem(z + k, NZ)
        z_copies.append(
            remote(w, wfull.at[z, xy, d], wz_send.at[k], wz_recv.at[k], (to * 4 + xy, d))
        )
    for c in z_copies:
        c.start()

    nb = min(256, CQ)
    cot_cat = jnp.concatenate([cot[:, q * VQ:(q + 1) * VQ] for q in range(Q)], 0)
    cot_rows = jnp.dot(de[...], cot_cat, preferred_element_type=F32).astype(BF16)
    cot_rows = cot_rows.reshape(F, rows, VQ)
    for dd in range(D):
        for n in range(CQ // nb):
            piece = jnp.concatenate(
                [tok[:, dd * MD + q * CQ + n * nb:dd * MD + q * CQ + (n + 1) * nb] for q in range(Q)], 0
            )
            out = jnp.dot(de[...], piece, preferred_element_type=F32).astype(BF16)
            send[dd, :, :, n * nb:(n + 1) * nb] = out.reshape(F, rows, nb)
        send[dd, :, :, CQ:] = cot_rows

        @pl.loop(0, F // 2)
        def _(k):
            a = (1 - f // (F // 2)) * (F // 2) + lax.rem(f + k, F // 2)
            remote(send.at[dd, a], recv.at[me], send_sem, recv_sem, (a, dd)).start()

    for dd in range(D):

        @pl.loop(0, F // 2)
        def _(k):
            a = (f // (F // 2)) * (F // 2) + lax.rem(f + k, F // 2)
            is_me = jnp.logical_and(a == f, d == dd)

            @pl.when(is_me)
            def _():
                pltpu.make_async_copy(send.at[dd, a], recv.at[me], recv_sem).start()

            @pl.when(jnp.logical_not(is_me))
            def _():
                remote(send.at[dd, a], recv.at[me], send_sem, recv_sem, (a, dd)).start()

    own_w.wait()
    for c in z_copies:
        c.wait()
    xn, yn = xy + 1 - 2 * (xy % 2), lax.rem(xy + 2, 4)
    line = lambda p: wfull.at[:, p, d]
    p_copies = [
        remote(line(xy), line(xy), wp_send.at[0], wp_recv.at[0], (z * 4 + xn, d)),
        remote(line(xy), line(xy), wp_send.at[1], wp_recv.at[1], (z * 4 + yn, d)),
    ]
    for c in p_copies:
        c.start()
    s_copies = []

    def share(p, slot):
        for k in range(1, D):
            c = remote(
                line(p), line(p), ws_send.at[slot, k], ws_recv.at[slot, k], (f, lax.rem(d + k, D))
            )
            c.start()
            s_copies.append(c)

    share(xy, 0)
    half = NZ // 2
    top = lambda p: wfull.at[0:half, p, d]
    low_half = lambda p: wfull.at[half:NZ, p, d]
    p_copies[0].wait()
    c2 = remote(top(xn), top(xn), wp_send.at[2], wp_recv.at[2], (z * 4 + yn, d))
    c2.start()
    share(xn, 1)
    p_copies[1].wait()
    c3 = remote(low_half(yn), low_half(yn), wp_send.at[3], wp_recv.at[3], (z * 4 + xn, d))
    c3.start()
    share(yn, 2)

    pltpu.make_async_copy(recv, recv, recv_sem).wait()
    G = GROUP
    gr, gc = G * rows, G * capp

    def gather_rows(x):
        x = x * mask[...]
        hi = x.astype(BF16)
        r1 = x - hi.astype(F32)
        mid = r1.astype(BF16)
        lo = (r1 - mid.astype(F32)).astype(BF16)
        y = jnp.dot(s8[...], hi, preferred_element_type=F32)
        y = y + jnp.dot(s8[...], mid, preferred_element_type=F32)
        y = y + jnp.dot(s8[...], lo, preferred_element_type=F32)
        return sum([y[:, q * R:(q + 1) * R] for q in range(Q)])

    def spread_rows(x):
        x = jnp.concatenate([x] * Q, 1)
        return (jnp.dot(s8t[...], x, preferred_element_type=F32) * mask[...]).astype(BF16)

    @pl.loop(0, N // G)
    def _(g):
        x = recv[pl.ds(g * G, G), :, 0:CQ].reshape(gr, CQ)
        p = gather_rows(jnp.dot(x, dn[...], preferred_element_type=F32))
        part[d, pl.ds(pl.multiple_of(g * gc, 8), gc), :] = jnp.concatenate([p] * (128 // R), 1)
        c = recv[pl.ds(g * G, G), :, CQ:C].reshape(gr, VQ)
        rc = gather_rows(jnp.dot(c, upq[...], preferred_element_type=F32)).astype(BF16)
        re[g] = spread_rows(rc)

    pt_copies = [
        remote(part.at[d], part.at[d], pt_send.at[k], pt_recv.at[k], (f, lax.rem(d + k, D)))
        for k in range(1, D)
    ]
    for c in pt_copies:
        c.start()
    for c in pt_copies:
        c.wait()
    gu[...] = jnp.zeros_like(gu)

    @pl.loop(0, N // G)
    def _(g):
        at = pl.ds(pl.multiple_of(g * gc, 8), gc)
        low = sum([part[k, at, 0:R] for k in range(D)]).astype(BF16)
        le = spread_rows(low)
        ret[pl.ds(g * G, G)] = (
            jnp.dot(le, upst[...], preferred_element_type=F32).astype(BF16).reshape(G, rows, VQ)
        )
        c = recv[pl.ds(g * G, G), :, CQ:C].reshape(gr, VQ)
        gu[...] += lax.dot_general(le, c, (((0,), (0,)), ((), ())), preferred_element_type=F32)

    @pl.loop(0, F)
    def _(k):
        s = lax.rem(f + k, F)

        @pl.when(s == f)
        def _():
            pltpu.make_async_copy(ret.at[s * D + d], back.at[f], rt_recv).start()

        @pl.when(s != f)
        def _():
            remote(ret.at[s * D + d], back.at[f], rt_send, rt_recv, (s, d)).start()

    c2.wait()
    c3.wait()
    share(3 - xy, 3)

    gd[...] = jnp.zeros_like(gd)

    @pl.loop(0, N // G)
    def _(g):
        x = recv[pl.ds(g * G, G), :, 0:CQ].reshape(gr, CQ)
        gd[...] += lax.dot_general(x, re[g], (((0,), (0,)), ((), ())), preferred_element_type=F32)

    for c in s_copies:
        c.wait()

    total = jnp.broadcast_to(bias[...].astype(F32), (tok.shape[0], V))
    M = tok.shape[1]
    steps = NZ
    kk = M // steps
    for i in range(steps):
        block = wfull[i].reshape(kk, V)
        total = total + jnp.dot(tok[:, i * kk:(i + 1) * kk], block, preferred_element_type=F32)

    pltpu.make_async_copy(back, back, rt_recv).wait()
    T = tok.shape[0]
    b = back[...].reshape(F * rows, VQ)
    placed = lax.dot_general(de[...], b, (((0,), (0,)), ((), ())), preferred_element_type=F32)
    placed = jnp.concatenate([placed[q * T:(q + 1) * T] for q in range(Q)], 1)
    values[...] = (total + placed).astype(BF16)

    pltpu.make_async_copy(recv.at[0:N - 1], recv.at[0:N - 1], send_sem).wait()
    pltpu.make_async_copy(back.at[0:F - 1], back.at[0:F - 1], rt_send).wait()


def body(tokens, token_adapter_index, adapter_storage_index, weight, bias, down, up, cotangent):
    F, D = lax.axis_size("fsdp"), lax.axis_size("dp")
    T, M = tokens.shape
    V = weight.shape[1]
    A = adapter_storage_index.shape[0]
    R = down.shape[2]
    Q = PIECES
    N = F * D
    cap = max(2, (3 * T + 2 * F - 1) // (2 * F))
    capp = -(-cap // Q) * Q
    rows = Q * capp
    MD, VQ = M // D, V // Q
    CQ = MD // Q
    NZ = F // 4
    d = lax.axis_index("dp")

    hot = token_adapter_index == jnp.arange(A)[None, :]
    owner = jnp.sum(jnp.where(hot, adapter_storage_index[None, :], 0), 1)
    i = jnp.arange(T)
    same = (owner[:, None] == owner[None, :]) & (i[None, :] < i[:, None])
    target = owner * capp + jnp.sum(same.astype(jnp.int32), 1)
    code = jnp.arange(A)[:, None, None] * capp + jnp.arange(capp)[None, None, :]
    code = jnp.broadcast_to(code, (A, Q, capp)).reshape(A * rows, 1, 1)
    q_row = jnp.broadcast_to(jnp.arange(Q)[None, :, None], (A, Q, capp)).reshape(A * rows, 1, 1)
    de = (code == target[None, None, :]) & (q_row == jnp.arange(Q)[None, :, None])
    de = de.astype(BF16).reshape(A * rows, Q * T)

    mine = lax.dynamic_slice_in_dim(down[0], d * MD, MD, 0)
    dn = mine.reshape(Q, CQ, R).transpose(1, 0, 2).reshape(CQ, Q * R)
    upst = up[0].reshape(R, Q, VQ).transpose(1, 0, 2).reshape(Q * R, VQ)
    upq = upst.T

    gr, gc = GROUP * rows, GROUP * capp
    rr, cc = np.arange(gr), np.arange(gc)
    from_row = (rr // rows) * capp + rr % capp
    s8t = (from_row[:, None] == cc[None, :]).astype(BF16)
    s8 = s8t.T
    mask = (((rr % rows) // capp)[:, None] == (np.arange(Q * R) // R)[None, :]).astype(np.float32)

    vmem = pl.BlockSpec(memory_space=pltpu.VMEM)
    dma = pltpu.SemaphoreType.DMA
    values, gd, gu = pl.pallas_call(
        functools.partial(kernel, F, D, NZ),
        out_shape=(
            jax.ShapeDtypeStruct((T, V), BF16),
            jax.ShapeDtypeStruct((CQ, Q * R), F32),
            jax.ShapeDtypeStruct((Q * R, VQ), F32),
        ),
        in_specs=[vmem] * 11,
        out_specs=(vmem,) * 3,
        scratch_shapes=[
            pltpu.VMEM((D, F, rows, CQ + VQ), BF16),
            pltpu.VMEM((N, rows, CQ + VQ), BF16),
            pltpu.VMEM((NZ, 4, D, M // N, V), BF16),
            pltpu.VMEM((D, N * capp, 128), F32),
            pltpu.VMEM((N // GROUP, gr, Q * R), BF16),
            pltpu.VMEM((N, rows, VQ), BF16),
            pltpu.VMEM((F, rows, VQ), BF16),
            dma, dma,
            dma((NZ,)), dma((NZ,)),
            dma((4,)), dma((4,)),
            dma((4, D)), dma((4, D)),
            dma((D,)), dma((D,)),
            dma, dma,
        ],
        compiler_params=pltpu.CompilerParams(
            collective_id=0, has_side_effects=True, vmem_limit_bytes=56 * 2**20
        ),
    )(tokens, de, cotangent, weight, dn, upq, upst, s8, s8t, mask, bias[None, :])
    gd = gd.reshape(CQ, Q, R).transpose(1, 0, 2).reshape(1, MD, R)
    gu = gu.reshape(Q, R, VQ).transpose(1, 0, 2).reshape(R, V)
    gu = lax.dynamic_slice_in_dim(gu, d * (V // D), V // D, 1)[None]
    return values, gd, gu


def solution(mesh):
    return jax.shard_map(
        body,
        mesh=mesh,
        in_specs=(
            P(("fsdp", "dp"), None),
            P(("fsdp", "dp"), None),
            P(),
            P(("fsdp", "dp"), None),
            P(),
            P("fsdp", None, None),
            P("fsdp", None, None),
            P(("fsdp", "dp"), None),
        ),
        out_specs=(P(("fsdp", "dp"), None), P("fsdp", "dp", None), P("fsdp", None, "dp")),
        check_vma=False,
    )
```
